32 devices in a mesh: grp: 4 (over x, core), wav: 8 (over z, y).
Axes of the slice: x: 2, y: 2, z: 4, core: 2. Of those that a mesh axis runs over, the one named last changes fastest.
Arguments:
- spectra: float32 [3, 8, 16, 2, 2560], P(None, 'grp', 'wav'), may hold values from -6 to 6
- legendre: float32 [16, 2560, 32], P('wav'), may hold values from -0.03125 to 0.03125
- wave_number: int32 [16], replicated, may hold values from 0 to 2559, as said below
- cycle_points: int32 [32], replicated, may hold values from 20 to 10256, as said below
- cycle_owner: int32 [64], replicated, may hold values from 0 to 63, each once
Outputs:
- grid_columns: float32 [64, 3, 8, 11264], P('grp', None, None, 'wav')
The draws below stay inside these ranges and needn't reach their ends.
Inputs may be any that keep to these rules, and one draw needn't show every extreme that they name: `wave_number`: all distinct; entries 2 i and 2 i + 1 sum to 2559. `cycle_points`: each is 20 + 4 k for a whole k, rising with the latitude index; 20 and 10256 both occur. `cycle_owner`: A permutation of the cycles: 0 to 31 northern, 32 + i the southern mirror of latitude i.
All inputs are finite; a program needn't handle non-finite values.
Results may differ from the reference program's by a relative error of at most 0.0003.
Values sent between devices are 32-bit elements; how exact they have to be, the bound alone decides.
A program may use at most 128 MiB of HBM per device.

```python
import jax
import jax.numpy as jnp
from jax import lax

NTR = 2560
RMAX = 10256
MW = 16
NH = 32
NR = 64
LEV = 8
PAD = 11264


def draw_wave_number(key, part):
    half_count = MW // 2
    first_key, second_key = jax.random.split(jax.random.fold_in(key, 11))
    others = 1 + jax.random.permutation(first_key, NTR // 2 - 1)[:half_count - 1]
    lowest = jnp.concatenate([jnp.zeros((1,), jnp.int32), others.astype(jnp.int32)])
    lowest = lowest[jax.random.permutation(second_key, half_count)]
    paired = jnp.stack([lowest, NTR - 1 - lowest], axis=1).reshape(MW)
    return paired.astype(jnp.int32)


def draw_cycle_points(key, part):
    top_index = (RMAX - 20) // 4
    inner = 1 + jax.random.permutation(jax.random.fold_in(key, 23), top_index - 1)[:NH - 2]
    ends = jnp.array([0, top_index], dtype=jnp.int32)
    ordered = jnp.sort(jnp.concatenate([ends, inner.astype(jnp.int32)]))
    return (20 + 4 * ordered).astype(jnp.int32)


def shard_levels(stream_key, dims, shards, low, high):
    gain = 1.0
    for position, blocks in shards:
        steps = jax.random.uniform(jax.random.fold_in(jax.random.fold_in(stream_key, 6), position), (blocks,), jnp.float32, low / len(shards), high / len(shards))
        gain = gain * jnp.repeat(jnp.exp(steps), dims[position] // blocks).reshape((-1,) + (1,) * (len(dims) - 1 - position))
    return gain


def scatter_about(own_key, extent, spread, reach, cuts=(), kind=jnp.bfloat16):
    factor_of = shard_levels(own_key, extent, cuts, -0.22, 0.18) if cuts else 1.0
    values = jax.random.normal(own_key, extent, jnp.float32) * spread * factor_of
    return jnp.minimum(jnp.maximum(values, -reach), reach).astype(kind)


def setup_inputs(seed: int = 0) -> dict:
    key_of = jax.random.split(jax.random.key(seed), 6)
    spectra = scatter_about(key_of[0], (3, LEV, MW, 2, NTR), 1.0, 6.0, ((1, 4), (2, 8)), jnp.float32)
    legendre = scatter_about(key_of[1], (MW, NTR, NH), (NTR * MW) ** -0.5, 0.03125, ((0, 8),), jnp.float32)
    wave_number = draw_wave_number(jax.random.fold_in(key_of[5], 71), 0)
    cycle_points = draw_cycle_points(jax.random.fold_in(key_of[5], 71), 0)
    cycle_owner = jax.random.permutation(key_of[4], NR).astype(jnp.int32)
    return {"spectra": spectra, "legendre": legendre, "wave_number": wave_number, "cycle_points": cycle_points, "cycle_owner": cycle_owner}


TWO_PI = 6.283185307179586
HIGHEST = lax.Precision.HIGHEST


def synthesis(coeffs, wave_list, lengths, offset, points_count):
    points = offset + jnp.arange(points_count, dtype=jnp.int32)
    weight = jnp.where(wave_list == 0, 1.0, 2.0).astype(jnp.float32)
    wave_total = wave_list.shape[0]

    def one_cycle(cycle_args):
        cycle_block, cycle_length = cycle_args
        phases = (wave_list[:, None] * points[None, :]) % cycle_length
        angles = phases.astype(jnp.float32) * (TWO_PI / cycle_length.astype(jnp.float32))
        cosine = weight[:, None] * jnp.cos(angles)
        sine_part = -weight[:, None] * jnp.sin(angles)
        fourier_basis = jnp.stack([cosine, sine_part], axis=1).reshape(2 * wave_total, points_count)
        flattened = cycle_block.reshape(-1, 2 * wave_total)
        values = jnp.dot(flattened, fourier_basis, precision=HIGHEST, preferred_element_type=jnp.float32)
        values = jnp.where(points[None, :] < cycle_length, values, 0.0)
        return values.reshape(cycle_block.shape[:-1] + (points_count,))

    return lax.map(one_cycle, (coeffs, lengths))


def reference(spectra, legendre, wave_number, cycle_points, cycle_owner):
    offsets = jnp.arange(NTR, dtype=jnp.int32)
    inside = (wave_number[:, None] + offsets[None, :]) < NTR
    masked = jnp.where(inside[None, None, :, None, :], spectra, 0.0)
    parity_signs = jnp.where(offsets % 2 == 0, 1.0, -1.0).astype(jnp.float32)

    def one_wave(wave_args):
        coefficients, wave_table = wave_args
        mirrored = jnp.concatenate([wave_table, wave_table * parity_signs[:, None]], axis=1)
        return jnp.einsum("flck,kr->flcr", coefficients, mirrored, precision=HIGHEST)

    fourier = lax.map(one_wave, (jnp.moveaxis(masked, 2, 0), legendre))
    placed = jnp.take(fourier, cycle_owner, axis=4)
    rows_first = jnp.transpose(placed, (4, 1, 2, 0, 3)).reshape(NR, 3, LEV, 2 * MW)
    cycle_lengths = jnp.concatenate([cycle_points, cycle_points])[cycle_owner]
    return synthesis(rows_first, wave_number, cycle_lengths, 0, PAD)
```

```python
import functools
import math

import jax
import jax.numpy as jnp
from jax import lax
from jax.experimental import pallas as pl
from jax.experimental.pallas import tpu as pltpu
from jax.sharding import PartitionSpec as P

RMAX = 10256
SLOTS = 8
NEAR = 256
VMEM_BYTES = 24000 * 2**10
MESH = pl.DeviceIdType.MESH


def iota(shape, dim):
    return lax.broadcasted_iota(jnp.int32, shape, dim)


def split(x):
    high = x.astype(jnp.bfloat16)
    return high, (x - high.astype(jnp.float32)).astype(jnp.bfloat16)


def dot(a, b, dims=((1,), (0,))):
    return lax.dot_general(a, b, (dims, ((), ())), preferred_element_type=jnp.float32)


def one_hot(mask):
    return mask.astype(jnp.float32).astype(jnp.bfloat16)


def reduced(x, length, inverse):
    turns = jnp.floor(x.astype(jnp.float32) * inverse).astype(jnp.int32)
    left = x - turns * length
    left = jnp.where(left < 0, left + length, left)
    return jnp.where(left >= length, left - length, left)


def cosine(x, length, inverse):
    left = reduced(x, length, inverse)
    left = jnp.where(2 * left > length, left - length, left)
    half = left.astype(jnp.float32) * (inverse * math.pi)
    square = half * half
    series = jnp.full_like(square, 1.0 / math.factorial(13))
    for power in (11, 9, 7, 5, 3, 1):
        sign = -1.0 if power % 4 == 3 else 1.0
        series = series * square + sign / math.factorial(power)
    sine = series * half
    return 1.0 - 2.0 * sine * sine


def routing(owner, half, lanes):
    lane_row = iota((1, lanes), 1) // SLOTS
    cycle = jnp.zeros((1, lanes), jnp.int32)
    for row in range(2 * half):
        cycle = jnp.where(lane_row == row, owner[row], cycle)
    latitude = iota((half, lanes), 0)
    north, south = one_hot(latitude == cycle), one_hot(latitude + half == cycle)
    return jnp.concatenate([north, north, south, south], axis=0)


def tables(columns, count, segment, wide, wave, points, owner, basis, turn, cross, limit):
    depth = 4 * columns
    tile_rows = turn.shape[1]
    g, w = lax.axis_index("grp"), lax.axis_index("wav")
    half = points.shape[0]
    deep = iota((depth, NEAR), 0)
    deep_wave = jnp.zeros((depth, NEAR), jnp.int32)
    across = iota((tile_rows, wide), 1) % depth
    across_wave = jnp.zeros((tile_rows, wide), jnp.int32)
    for q in range(depth // 2):
        deep_wave = jnp.where(deep // 2 == q, wave[q], deep_wave)
        across_wave = jnp.where(across // 2 == q, wave[q], across_wave)
    near = deep_wave * iota((depth, NEAR), 1)
    far = across_wave * (w * segment + NEAR * iota((tile_rows, wide), 0))
    weight = jnp.where(across_wave == 0, 1.0, 2.0)
    point = iota((8, 128), 1) + w * segment

    @pl.loop(0, count, unroll=count if count <= 16 else 1)
    def _(p):
        length = points[lax.rem(owner[g * count + p], half)]
        quarter = lax.div(length, 4)
        inverse = 1.0 / jnp.full((1, 128), length, jnp.int32).astype(jnp.float32)
        across_near = jnp.concatenate([inverse] * (NEAR // 128), axis=1)
        high, low = split(cosine(near + (deep % 2) * quarter, length, across_near))
        basis[p, :depth] = high
        basis[p, depth:] = low
        inverse = jnp.concatenate([inverse] * (wide // 128), axis=1)
        turn[p] = weight * cosine(far, length, inverse)
        cross[p] = weight * cosine(far + (1 + 2 * (across % 2)) * quarter, length, inverse)
        limit[p] = length - point


def spread(groups, columns, segment, wide, *refs):
    spec_in, leg_in, wave_in, points_in, owner_in = refs[:5]
    out, basis, turn, cross, limit = refs[5:10]
    spec, leg, wave, points, owner, send, send_sem, recv_sem, load_sem = refs[10:]
    devices = groups * columns
    g, w = lax.axis_index("grp"), lax.axis_index("wav")
    me = w * groups + g
    waves, half, degrees = leg.shape
    lanes = send.shape[2]
    count = basis.shape[0]
    steps = degrees // 128
    fields, levels = spec_in.shape[:2]
    rows = 2 * fields * levels

    barrier = pltpu.get_barrier_semaphore()
    small = [
        pltpu.make_async_copy(wave_in, wave, load_sem.at[0]),
        pltpu.make_async_copy(points_in, points, load_sem.at[1]),
        pltpu.make_async_copy(owner_in, owner, load_sem.at[2]),
    ]
    large = [pltpu.make_async_copy(spec_in, spec, load_sem.at[3])]
    for q in range(waves):
        large.append(pltpu.make_async_copy(leg_in.at[q], leg.at[q], load_sem.at[4 + q]))
    for load in small + large:
        load.start()

    def each(act):
        @pl.loop(0, devices - 1, unroll=devices - 1 if devices <= 32 else 1)
        def _(i):
            to = i + (me <= i).astype(jnp.int32)
            act(lax.rem(to, groups), lax.div(to, groups))

    each(lambda *to: pl.semaphore_signal(barrier, inc=1, device_id=to, device_id_type=MESH))
    for load in small:
        load.wait()
    pick = routing(owner, half, groups * lanes)
    sign = jnp.where(iota((16, degrees), 1) % 2 == 0, 1.0, -1.0).astype(jnp.bfloat16)[:1]

    large[0].wait()
    parts = []
    for q in range(waves):
        number = wave[w * waves + q]
        inside = iota((16, degrees), 1) + jnp.where(iota((16, degrees), 0) < rows, number, degrees) < degrees
        high, low = split(jnp.where(inside, jnp.concatenate([spec[f, l, q] for f in range(fields) for l in range(levels)] + [jnp.zeros((16 - rows, degrees), jnp.float32)], axis=0), 0.0))
        large[1 + q].wait()
        table = jnp.concatenate(split(leg[q]), axis=0)
        table = jnp.concatenate([table, table * sign], axis=0)
        both = dot(jnp.concatenate([high, low], axis=0), table, ((1,), (1,)))
        parts.append(both[:16] + both[16:])
    fourier = jnp.concatenate(parts, axis=0)
    moved = dot(jnp.concatenate(split(fourier), axis=0), pick)
    height = fourier.shape[0]
    moved = moved[:height] + moved[height:]
    slot = iota((16, groups * lanes), 1) % SLOTS == iota((16, groups * lanes), 0) // 2
    message = jnp.zeros((8, groups * lanes), jnp.float32)
    for q in range(waves):
        kept = jnp.where(slot, moved[16 * q : 16 * q + 16], 0.0)
        kept = kept[:8] + kept[8:]
        kept = kept + pltpu.roll(kept, 4, 0)
        kept = kept + pltpu.roll(kept, 2, 0)
        message = jnp.where(iota(message.shape, 0) // 2 == q, kept, message)
    for to in range(groups):
        send[to] = message[:4, to * lanes : (to + 1) * lanes]
    out[g * columns + w] = send[g]

    pl.semaphore_wait(barrier, devices - 1)

    def start(to_g, to_w):
        pltpu.make_async_remote_copy(
            src_ref=send.at[to_g],
            dst_ref=out.at[g * columns + w],
            send_sem=send_sem,
            recv_sem=recv_sem,
            device_id=(to_g, to_w),
            device_id_type=MESH,
        ).start()

    each(start)
    tables(columns, count, segment, wide, wave, points, owner, basis, turn, cross, limit)
    others = out.at[pl.ds(0, devices - 1)]
    pltpu.make_async_copy(others, others, send_sem).wait()
    pltpu.make_async_copy(others, others, recv_sem).wait()


def swap(x):
    even = iota(x.shape, 0) % 2 == 0
    return jnp.where(even, pltpu.roll(x, x.shape[0] - 1, 0), pltpu.roll(x, 1, 0))


def by_field(groups, columns, fields, levels, got):
    depth, lanes = 4 * columns, got.shape[2]
    x = [got[i * columns : (i + 1) * columns].reshape(depth, lanes) for i in range(groups)]
    source = iota((depth, lanes), 1) % SLOTS // levels
    placed = []
    for f in range(fields):
        total = jnp.zeros((depth, lanes), jnp.float32)
        for i in range(groups):
            shift = (i - f) * levels % lanes
            total = jnp.where(source == i, pltpu.roll(x[i], shift, 1) if shift else x[i], total)
        placed.append(total)
    return placed


def arrange(groups, columns, copies, got, coeffs):
    fields, height, _ = coeffs.shape
    depth, lanes = 4 * columns, got.shape[2]
    count = lanes // SLOTS
    level_total = height // count
    levels = level_total // groups
    if level_total == SLOTS:
        same = one_hot(iota((lanes, lanes), 0) == iota((lanes, lanes), 1))
        same = jnp.concatenate([same, same], axis=1)
        for f, x in enumerate(by_field(groups, columns, fields, levels, got)):
            own, other = split(x), split(swap(x))
            source = [jnp.concatenate([own[h]] * copies + [other[h]] * copies, axis=0) for h in range(2)]
            coeffs[f] = dot(same, jnp.concatenate(source, axis=1), ((1,), (1,)))
        return
    x = [got[i * columns : (i + 1) * columns].reshape(depth, lanes) for i in range(groups)]
    x = jnp.concatenate(x, axis=1)
    own, other = split(x), split(swap(x))
    source = [jnp.concatenate([own[h]] * copies + [other[h]] * copies, axis=0) for h in range(2)]
    target = iota((height, 1), 0)
    level = lax.rem(target, level_total)
    for f in range(fields):
        at = (
            lax.div(level, levels) * lanes
            + lax.div(target, level_total) * SLOTS
            + f * levels
            + lax.rem(level, levels)
        )
        move = one_hot(iota((height, groups * lanes), 1) == at)
        coeffs[f] = dot(move, source[0], ((1,), (1,))) + dot(move, source[1], ((1,), (1,)))


def synthesis(groups, columns, got, basis, turn, cross, limit, out, coeffs, grid, out_sem):
    depth = 4 * columns
    count, fields, level_total, segment = grid.shape
    block = fields * level_total
    wide = turn.shape[2]
    copies = wide // depth
    tiles = -(-segment // NEAR)
    arrange(groups, columns, copies, got, coeffs)
    rest = (iota((block * tiles, wide), 1) // depth) % 2 == 1

    def write(p):
        return pltpu.make_async_copy(grid.at[p], out.at[p], out_sem.at[p])

    @pl.loop(0, count, unroll=16)
    def _(p):
        at = pl.ds(pl.multiple_of(p * level_total, 8), level_total)
        own = jnp.concatenate([coeffs[f, at, :wide] for f in range(fields)], axis=0)
        other = jnp.concatenate([coeffs[f, at, wide:] for f in range(fields)], axis=0)
        turns, crosses = turn[p], cross[p]
        turned = jnp.concatenate(
            [own * turns[t : t + 1] + other * crosses[t : t + 1] for t in range(tiles)], axis=0
        )
        head = turned.astype(jnp.bfloat16).astype(jnp.float32)
        parts = jnp.where(rest, turned - head, head).astype(jnp.bfloat16)
        high, low = basis[p, :depth], basis[p, depth:]
        values = dot(parts, jnp.concatenate([high, high, low, low][:copies], axis=0))
        room = limit[p]
        room = jnp.concatenate([room] * (level_total // 8), axis=0)
        for start in range(0, segment, 128):
            t, lane = start // NEAR, start % NEAR
            inside = room > start
            for f in range(fields):
                at = t * block + f * level_total
                kept = values[at : at + level_total, lane : lane + 128]
                grid[p, f, :, start : start + 128] = jnp.where(inside, kept, 0.0)
        write(p).start()

    @pl.loop(0, count)
    def _(p):
        write(p).wait()


def body(groups, columns, spectra, legendre, wave_number, cycle_points, cycle_owner):
    fields, levels, waves, parts, degrees = spectra.shape
    half = legendre.shape[2]
    count = 2 * half // groups
    lanes = count * SLOTS
    level_total = levels * groups
    depth = waves * 2 * columns
    segment = (RMAX + 128 * columns - 1) // (128 * columns) * 128
    wide = -(-3 * depth // 128) * 128
    tile_rows = -(-(-(-segment // NEAR)) // 8) * 8
    vmem, hbm = pl.BlockSpec(memory_space=pltpu.VMEM), pl.BlockSpec(memory_space=pltpu.HBM)
    inputs = (spectra, jnp.swapaxes(legendre, 1, 2), wave_number, cycle_points, cycle_owner)
    handed = pl.pallas_call(
        functools.partial(spread, groups, columns, segment, wide),
        out_shape=[
            pltpu.VMEM((groups * columns, 4, lanes), jnp.float32),
            pltpu.VMEM((count, 2 * depth, NEAR), jnp.bfloat16),
            pltpu.VMEM((count, tile_rows, wide), jnp.float32),
            pltpu.VMEM((count, tile_rows, wide), jnp.float32),
            pltpu.VMEM((count, 8, 128), jnp.int32),
        ],
        in_specs=[hbm] * 5,
        out_specs=[vmem] * 5,
        scratch_shapes=[
            pltpu.VMEM(spectra.shape, jnp.float32),
            pltpu.VMEM((waves, half, degrees), jnp.float32),
            pltpu.SMEM(wave_number.shape, jnp.int32),
            pltpu.SMEM(cycle_points.shape, jnp.int32),
            pltpu.SMEM(cycle_owner.shape, jnp.int32),
            pltpu.VMEM((groups, 4, lanes), jnp.float32),
            pltpu.SemaphoreType.DMA,
            pltpu.SemaphoreType.DMA,
            pltpu.SemaphoreType.DMA((4 + waves,)),
        ],
        compiler_params=pltpu.CompilerParams(
            collective_id=0, has_side_effects=True, vmem_limit_bytes=VMEM_BYTES
        ),
        name="spread",
    )(*[pltpu.with_memory_space_constraint(x, pltpu.HBM) for x in inputs])
    return pl.pallas_call(
        functools.partial(synthesis, groups, columns),
        out_shape=jax.ShapeDtypeStruct((count, fields, level_total, segment), jnp.float32),
        in_specs=[vmem] * 5,
        out_specs=pl.BlockSpec(memory_space=pl.ANY),
        scratch_shapes=[
            pltpu.VMEM((fields, count * level_total, 2 * wide), jnp.float32),
            pltpu.VMEM((count, fields, level_total, segment), jnp.float32),
            pltpu.SemaphoreType.DMA((count,)),
        ],
        compiler_params=pltpu.CompilerParams(vmem_limit_bytes=VMEM_BYTES),
        name="synthesis",
    )(*[pltpu.with_memory_space_constraint(x, pltpu.VMEM) for x in handed])


def solution(mesh):
    in_specs = (P(None, "grp", "wav", None, None), P("wav", None, None), P(), P(), P())
    out_specs = P("grp", None, None, "wav")
    groups, columns = mesh.shape["grp"], mesh.shape["wav"]
    return jax.shard_map(
        functools.partial(body, groups, columns),
        mesh=mesh,
        in_specs=in_specs,
        out_specs=out_specs,
        check_vma=False,
    )
```

```python
import functools
import math

import jax
import jax.numpy as jnp
from jax import lax
from jax.experimental import pallas as pl
from jax.experimental.pallas import tpu as pltpu
from jax.sharding import PartitionSpec as P

RMAX = 10256
SLOTS = 8
NEAR = 256
VMEM_BYTES = 24000 * 2**10
MESH = pl.DeviceIdType.MESH


def iota(shape, dim):
    return lax.broadcasted_iota(jnp.int32, shape, dim)


def split(x):
    high = x.astype(jnp.bfloat16)
    return high, (x - high.astype(jnp.float32)).astype(jnp.bfloat16)


def dot(a, b, dims=((1,), (0,))):
    return lax.dot_general(a, b, (dims, ((), ())), preferred_element_type=jnp.float32)


def one_hot(mask):
    return mask.astype(jnp.float32).astype(jnp.bfloat16)


def reduced(x, length, inverse):
    turns = jnp.floor(x.astype(jnp.float32) * inverse).astype(jnp.int32)
    left = x - turns * length
    left = jnp.where(left < 0, left + length, left)
    return jnp.where(left >= length, left - length, left)


def cosine(x, length, inverse):
    left = reduced(x, length, inverse)
    left = jnp.where(2 * left > length, left - length, left)
    half = left.astype(jnp.float32) * (inverse * math.pi)
    square = half * half
    series = jnp.full_like(square, 1.0 / math.factorial(13))
    for power in (11, 9, 7, 5, 3, 1):
        sign = -1.0 if power % 4 == 3 else 1.0
        series = series * square + sign / math.factorial(power)
    sine = series * half
    return 1.0 - 2.0 * sine * sine


def routing(owner, half, groups, lanes):
    count = 2 * half // groups
    lane_row = iota((1, count * SLOTS), 1) // SLOTS
    cycles = []
    for to in range(groups):
        cycle = jnp.zeros(lane_row.shape, jnp.int32)
        for row in range(count):
            cycle = jnp.where(lane_row == row, owner[to * count + row], cycle)
        cycles.append(cycle)
    cycle = jnp.concatenate(cycles, axis=1)
    latitude = iota((half, lanes), 0)
    north, south = one_hot(latitude == cycle), one_hot(latitude + half == cycle)
    return jnp.concatenate([north, north, south, south], axis=0)


def tables(columns, count, segment, wide, wave, points, owner, basis, turn, cross, limit):
    depth = 4 * columns
    tile_rows = turn.shape[1]
    g, w = lax.axis_index("grp"), lax.axis_index("wav")
    half = points.shape[0]
    deep = iota((depth, NEAR), 0)
    deep_wave = jnp.zeros((depth, NEAR), jnp.int32)
    across = iota((tile_rows, wide), 1) % depth
    across_wave = jnp.zeros((tile_rows, wide), jnp.int32)
    for q in range(depth // 2):
        deep_wave = jnp.where(deep // 2 == q, wave[q], deep_wave)
        across_wave = jnp.where(across // 2 == q, wave[q], across_wave)
    near = deep_wave * iota((depth, NEAR), 1)
    far = across_wave * (w * segment + NEAR * iota((tile_rows, wide), 0))
    weight = jnp.where(across_wave == 0, 1.0, 2.0)
    point = iota((8, 128), 1) + w * segment

    @pl.loop(0, count, unroll=count if count <= 16 else 1)
    def _(p):
        length = points[lax.rem(owner[g * count + p], half)]
        quarter = lax.div(length, 4)
        inverse = 1.0 / jnp.full((1, 128), length, jnp.int32).astype(jnp.float32)
        across_near = jnp.concatenate([inverse] * (NEAR // 128), axis=1)
        high, low = split(cosine(near + (deep % 2) * quarter, length, across_near))
        basis[p, :depth] = high
        basis[p, depth:] = low
        inverse = jnp.concatenate([inverse] * (wide // 128), axis=1)
        turn[p] = weight * cosine(far, length, inverse)
        cross[p] = weight * cosine(far + (1 + 2 * (across % 2)) * quarter, length, inverse)
        limit[p] = length - point


def spread(groups, columns, segment, wide, *refs):
    spec_in, leg_in, wave_in, points_in, owner_in = refs[:5]
    out, basis, turn, cross, limit = refs[5:10]
    spec, leg, wave, points, owner, send, send_sem, recv_sem, load_sem = refs[10:]
    devices = groups * columns
    g, w = lax.axis_index("grp"), lax.axis_index("wav")
    me = w * groups + g
    waves, half, degrees = leg.shape
    lanes = send.shape[2]
    count = basis.shape[0]
    steps = degrees // 128
    fields, levels = spec_in.shape[:2]
    rows = 2 * fields * levels

    barrier = pltpu.get_barrier_semaphore()
    small = [
        pltpu.make_async_copy(wave_in, wave, load_sem.at[0]),
        pltpu.make_async_copy(points_in, points, load_sem.at[1]),
        pltpu.make_async_copy(owner_in, owner, load_sem.at[2]),
    ]
    large = [pltpu.make_async_copy(spec_in, spec, load_sem.at[3])]
    for q in range(waves):
        large.append(pltpu.make_async_copy(leg_in.at[q], leg.at[q], load_sem.at[4 + q]))
    for load in small + large:
        load.start()

    def each(act):
        @pl.loop(0, devices - 1, unroll=devices - 1 if devices <= 32 else 1)
        def _(i):
            to = i + (me <= i).astype(jnp.int32)
            act(lax.rem(to, groups), lax.div(to, groups))

    each(lambda *to: pl.semaphore_signal(barrier, inc=1, device_id=to, device_id_type=MESH))
    for load in small:
        load.wait()
    pick = routing(owner, half, groups, groups * lanes)
    sign = jnp.where(iota((16, degrees), 1) % 2 == 0, 1.0, -1.0).astype(jnp.bfloat16)[:1]

    large[0].wait()
    stacks = []
    for q in range(waves):
        number = wave[w * waves + q]
        inside = iota((16, degrees), 1) + jnp.where(iota((16, degrees), 0) < rows, number, degrees) < degrees
        x = jnp.concatenate([spec[f, l, q] for f in range(fields) for l in range(levels)] + [jnp.zeros((16 - rows, degrees), jnp.float32)], axis=0)
        stacks.append(jnp.concatenate(split(jnp.where(inside, x, 0.0)), axis=0))
    for load in large[1:]:
        load.wait()
    parts = []
    for q in range(waves):
        table = jnp.concatenate(split(leg[q]), axis=0)
        table = jnp.concatenate([table, table * sign], axis=0)
        both = dot(stacks[q], table, ((1,), (1,)))
        parts.append(both[:16] + both[16:])
    fourier = jnp.concatenate(parts, axis=0)
    moved = dot(jnp.concatenate(split(fourier), axis=0), pick)
    height = fourier.shape[0]
    moved = moved[:height] + moved[height:]
    slot = iota((16, groups * lanes), 1) % SLOTS == iota((16, groups * lanes), 0) // 2
    message = jnp.zeros((8, groups * lanes), jnp.float32)
    for q in range(waves):
        kept = jnp.where(slot, moved[16 * q : 16 * q + 16], 0.0)
        kept = kept[:8] + kept[8:]
        kept = kept + pltpu.roll(kept, 4, 0)
        kept = kept + pltpu.roll(kept, 2, 0)
        message = jnp.where(iota(message.shape, 0) // 2 == q, kept, message)
    for to in range(groups):
        send[to] = message[:4, to * lanes : (to + 1) * lanes]
    out[g * columns + w] = send[g]

    pl.semaphore_wait(barrier, devices - 1)

    def start(to_g, to_w):
        pltpu.make_async_remote_copy(
            src_ref=send.at[to_g],
            dst_ref=out.at[g * columns + w],
            send_sem=send_sem,
            recv_sem=recv_sem,
            device_id=(to_g, to_w),
            device_id_type=MESH,
        ).start()

    each(start)
    tables(columns, count, segment, wide, wave, points, owner, basis, turn, cross, limit)
    others = out.at[pl.ds(0, devices - 1)]
    pltpu.make_async_copy(others, others, send_sem).wait()
    pltpu.make_async_copy(others, others, recv_sem).wait()


def swap(x):
    even = iota(x.shape, 0) % 2 == 0
    return jnp.where(even, pltpu.roll(x, x.shape[0] - 1, 0), pltpu.roll(x, 1, 0))


def by_field(groups, columns, fields, levels, got):
    depth, lanes = 4 * columns, got.shape[2]
    x = [got[i * columns : (i + 1) * columns].reshape(depth, lanes) for i in range(groups)]
    source = iota((depth, lanes), 1) % SLOTS // levels
    placed = []
    for f in range(fields):
        total = jnp.zeros((depth, lanes), jnp.float32)
        for i in range(groups):
            shift = (i - f) * levels % lanes
            total = jnp.where(source == i, pltpu.roll(x[i], shift, 1) if shift else x[i], total)
        placed.append(total)
    return placed


def arrange(groups, columns, copies, got, coeffs):
    fields, height, _ = coeffs.shape
    depth, lanes = 4 * columns, got.shape[2]
    count = lanes // SLOTS
    level_total = height // count
    levels = level_total // groups
    if level_total == SLOTS:
        same = one_hot(iota((lanes, lanes), 0) == iota((lanes, lanes), 1))
        same = jnp.concatenate([same, same], axis=1)
        for f, x in enumerate(by_field(groups, columns, fields, levels, got)):
            own, other = split(x), split(swap(x))
            source = [jnp.concatenate([own[h]] * copies + [other[h]] * copies, axis=0) for h in range(2)]
            coeffs[f] = dot(same, jnp.concatenate(source, axis=1), ((1,), (1,)))
        return
    x = [got[i * columns : (i + 1) * columns].reshape(depth, lanes) for i in range(groups)]
    x = jnp.concatenate(x, axis=1)
    own, other = split(x), split(swap(x))
    source = [jnp.concatenate([own[h]] * copies + [other[h]] * copies, axis=0) for h in range(2)]
    target = iota((height, 1), 0)
    level = lax.rem(target, level_total)
    for f in range(fields):
        at = (
            lax.div(level, levels) * lanes
            + lax.div(target, level_total) * SLOTS
            + f * levels
            + lax.rem(level, levels)
        )
        move = one_hot(iota((height, groups * lanes), 1) == at)
        coeffs[f] = dot(move, source[0], ((1,), (1,))) + dot(move, source[1], ((1,), (1,)))


def synthesis(groups, columns, got, basis, turn, cross, limit, out, coeffs, grid, out_sem):
    depth = 4 * columns
    count, fields, level_total, segment = grid.shape
    block = fields * level_total
    wide = turn.shape[2]
    copies = wide // depth
    tiles = -(-segment // NEAR)
    arrange(groups, columns, copies, got, coeffs)
    rest = (iota((block * tiles, wide), 1) // depth) % 2 == 1

    def write(p):
        return pltpu.make_async_copy(grid.at[p], out.at[p], out_sem.at[p])

    @pl.loop(0, count, unroll=16)
    def _(p):
        at = pl.ds(pl.multiple_of(p * level_total, 8), level_total)
        own = jnp.concatenate([coeffs[f, at, :wide] for f in range(fields)], axis=0)
        other = jnp.concatenate([coeffs[f, at, wide:] for f in range(fields)], axis=0)
        turns, crosses = turn[p], cross[p]
        turned = jnp.concatenate(
            [own * turns[t : t + 1] + other * crosses[t : t + 1] for t in range(tiles)], axis=0
        )
        head = turned.astype(jnp.bfloat16).astype(jnp.float32)
        parts = jnp.where(rest, turned - head, head).astype(jnp.bfloat16)
        high, low = basis[p, :depth], basis[p, depth:]
        values = dot(parts, jnp.concatenate([high, high, low, low][:copies], axis=0))
        room = limit[p]
        room = jnp.concatenate([room] * (level_total // 8), axis=0)
        for start in range(0, segment, 128):
            t, lane = start // NEAR, start % NEAR
            inside = room > start
            for f in range(fields):
                at = t * block + f * level_total
                kept = values[at : at + level_total, lane : lane + 128]
                grid[p, f, :, start : start + 128] = jnp.where(inside, kept, 0.0)
        write(p).start()

    @pl.loop(0, count)
    def _(p):
        write(p).wait()


def body(groups, columns, spectra, legendre, wave_number, cycle_points, cycle_owner):
    fields, levels, waves, parts, degrees = spectra.shape
    half = legendre.shape[2]
    count = 2 * half // groups
    lanes = count * SLOTS
    level_total = levels * groups
    depth = waves * 2 * columns
    segment = (RMAX + 128 * columns - 1) // (128 * columns) * 128
    wide = -(-3 * depth // 128) * 128
    tile_rows = -(-(-(-segment // NEAR)) // 8) * 8
    vmem, hbm = pl.BlockSpec(memory_space=pltpu.VMEM), pl.BlockSpec(memory_space=pltpu.HBM)
    inputs = (spectra, jnp.swapaxes(legendre, 1, 2), wave_number, cycle_points, cycle_owner)
    handed = pl.pallas_call(
        functools.partial(spread, groups, columns, segment, wide),
        out_shape=[
            pltpu.VMEM((groups * columns, 4, lanes), jnp.float32),
            pltpu.VMEM((count, 2 * depth, NEAR), jnp.bfloat16),
            pltpu.VMEM((count, tile_rows, wide), jnp.float32),
            pltpu.VMEM((count, tile_rows, wide), jnp.float32),
            pltpu.VMEM((count, 8, 128), jnp.int32),
        ],
        in_specs=[hbm] * 5,
        out_specs=[vmem] * 5,
        scratch_shapes=[
            pltpu.VMEM(spectra.shape, jnp.float32),
            pltpu.VMEM((waves, half, degrees), jnp.float32),
            pltpu.SMEM(wave_number.shape, jnp.int32),
            pltpu.SMEM(cycle_points.shape, jnp.int32),
            pltpu.SMEM(cycle_owner.shape, jnp.int32),
            pltpu.VMEM((groups, 4, lanes), jnp.float32),
            pltpu.SemaphoreType.DMA,
            pltpu.SemaphoreType.DMA,
            pltpu.SemaphoreType.DMA((4 + waves,)),
        ],
        compiler_params=pltpu.CompilerParams(
            collective_id=0, has_side_effects=True, vmem_limit_bytes=VMEM_BYTES
        ),
        name="spread",
    )(*[pltpu.with_memory_space_constraint(x, pltpu.HBM) for x in inputs])
    return pl.pallas_call(
        functools.partial(synthesis, groups, columns),
        out_shape=jax.ShapeDtypeStruct((count, fields, level_total, segment), jnp.float32),
        in_specs=[vmem] * 5,
        out_specs=pl.BlockSpec(memory_space=pl.ANY),
        scratch_shapes=[
            pltpu.VMEM((fields, count * level_total, 2 * wide), jnp.float32),
            pltpu.VMEM((count, fields, level_total, segment), jnp.float32),
            pltpu.SemaphoreType.DMA((count,)),
        ],
        compiler_params=pltpu.CompilerParams(vmem_limit_bytes=VMEM_BYTES),
        name="synthesis",
    )(*[pltpu.with_memory_space_constraint(x, pltpu.VMEM) for x in handed])


def solution(mesh):
    in_specs = (P(None, "grp", "wav", None, None), P("wav", None, None), P(), P(), P())
    out_specs = P("grp", None, None, "wav")
    groups, columns = mesh.shape["grp"], mesh.shape["wav"]
    return jax.shard_map(
        functools.partial(body, groups, columns),
        mesh=mesh,
        in_specs=in_specs,
        out_specs=out_specs,
        check_vma=False,
    )
```

```python
import functools
import math

import jax
import jax.numpy as jnp
from jax import lax
from jax.experimental import pallas as pl
from jax.experimental.pallas import tpu as pltpu
from jax.sharding import PartitionSpec as P

RMAX = 10256
SLOTS = 8
NEAR = 256
VMEM_BYTES = 24000 * 2**10
MESH = pl.DeviceIdType.MESH


def iota(shape, dim):
    return lax.broadcasted_iota(jnp.int32, shape, dim)


def split(x):
    high = x.astype(jnp.bfloat16)
    return high, (x - high.astype(jnp.float32)).astype(jnp.bfloat16)


def dot(a, b, dims=((1,), (0,))):
    return lax.dot_general(a, b, (dims, ((), ())), preferred_element_type=jnp.float32)


def one_hot(mask):
    return mask.astype(jnp.float32).astype(jnp.bfloat16)


def reduced(x, length, inverse):
    turns = jnp.floor(x.astype(jnp.float32) * inverse).astype(jnp.int32)
    left = x - turns * length
    left = jnp.where(left < 0, left + length, left)
    return jnp.where(left >= length, left - length, left)


def cosine(x, length, inverse):
    left = reduced(x, length, inverse)
    left = jnp.where(2 * left > length, left - length, left)
    half = left.astype(jnp.float32) * (inverse * math.pi)
    square = half * half
    series = jnp.full_like(square, 1.0 / math.factorial(13))
    for power in (11, 9, 7, 5, 3, 1):
        sign = -1.0 if power % 4 == 3 else 1.0
        series = series * square + sign / math.factorial(power)
    sine = series * half
    return 1.0 - 2.0 * sine * sine


def routing(owner, half, groups, lanes):
    count = 2 * half // groups
    lane_row = iota((1, count * SLOTS), 1) // SLOTS
    cycles = []
    for to in range(groups):
        cycle = jnp.zeros(lane_row.shape, jnp.int32)
        for row in range(count):
            cycle = jnp.where(lane_row == row, owner[to * count + row], cycle)
        cycles.append(cycle)
    cycle = jnp.concatenate(cycles, axis=1)
    latitude = iota((half, lanes), 0)
    north, south = one_hot(latitude == cycle), one_hot(latitude + half == cycle)
    return jnp.concatenate([north, north, south, south], axis=0)


def tables(columns, count, segment, wide, wave, points, owner, basis, turn, cross, limit):
    depth = 4 * columns
    tile_rows = turn.shape[1]
    g, w = lax.axis_index("grp"), lax.axis_index("wav")
    half = points.shape[0]
    deep = iota((depth, NEAR), 0)
    deep_wave = jnp.zeros((depth, NEAR), jnp.int32)
    across = iota((tile_rows, wide), 1) % depth
    across_wave = jnp.zeros((tile_rows, wide), jnp.int32)
    for q in range(depth // 2):
        deep_wave = jnp.where(deep // 2 == q, wave[q], deep_wave)
        across_wave = jnp.where(across // 2 == q, wave[q], across_wave)
    near = deep_wave * iota((depth, NEAR), 1)
    far = across_wave * (w * segment + NEAR * iota((tile_rows, wide), 0))
    weight = jnp.where(across_wave == 0, 1.0, 2.0)
    point = iota((8, 128), 1) + w * segment

    @pl.loop(0, count, unroll=count if count <= 16 else 1)
    def _(p):
        length = points[lax.rem(owner[g * count + p], half)]
        quarter = lax.div(length, 4)
        inverse = 1.0 / jnp.full((1, 128), length, jnp.int32).astype(jnp.float32)
        across_near = jnp.concatenate([inverse] * (NEAR // 128), axis=1)
        high, low = split(cosine(near + (deep % 2) * quarter, length, across_near))
        basis[p, :depth] = high
        basis[p, depth:] = low
        inverse = jnp.concatenate([inverse] * (wide // 128), axis=1)
        turn[p] = weight * cosine(far, length, inverse)
        cross[p] = weight * cosine(far + (1 + 2 * (across % 2)) * quarter, length, inverse)
        limit[p] = length - point


def spread(groups, columns, segment, wide, *refs):
    spec_in, leg_in, wave_in, points_in, owner_in = refs[:5]
    out, basis, turn, cross, limit = refs[5:10]
    spec, leg, wave, points, owner, send, send_sem, recv_sem, load_sem = refs[10:]
    devices = groups * columns
    g, w = lax.axis_index("grp"), lax.axis_index("wav")
    me = w * groups + g
    waves, half, degrees = leg.shape
    lanes = send.shape[2]
    count = basis.shape[0]
    steps = degrees // 128
    fields, levels = spec_in.shape[:2]
    rows = 2 * fields * levels

    barrier = pltpu.get_barrier_semaphore()
    small = [
        pltpu.make_async_copy(wave_in, wave, load_sem.at[0]),
        pltpu.make_async_copy(points_in, points, load_sem.at[1]),
        pltpu.make_async_copy(owner_in, owner, load_sem.at[2]),
    ]
    large = [pltpu.make_async_copy(spec_in, spec, load_sem.at[3])]
    large.append(pltpu.make_async_copy(leg_in, leg, load_sem.at[4]))
    for load in small + large:
        load.start()

    def each(act):
        @pl.loop(0, devices - 1, unroll=devices - 1 if devices <= 32 else 1)
        def _(i):
            to = i + (me <= i).astype(jnp.int32)
            act(lax.rem(to, groups), lax.div(to, groups))

    each(lambda *to: pl.semaphore_signal(barrier, inc=1, device_id=to, device_id_type=MESH))
    for load in small:
        load.wait()
    pick = routing(owner, half, groups, groups * lanes)
    sign = jnp.where(iota((16, 128), 1) % 2 == 0, 1.0, -1.0).astype(jnp.bfloat16)[:1]
    large[0].wait()
    halves = []
    for q in range(2):
        number = wave[w * waves + q]
        inside = iota((16, degrees), 1) + jnp.where(iota((16, degrees), 0) < rows, number, degrees) < degrees
        x = [spec[f, l, q] for f in range(fields) for l in range(levels)]
        x = jnp.concatenate(x + [jnp.zeros((16 - rows, degrees), jnp.float32)], axis=0)
        halves.append(split(jnp.where(inside, x, 0.0)))

    def tile(x, k):
        if 0 <= k < steps:
            return x[:, 128 * k : 128 * (k + 1)]
        return jnp.zeros((x.shape[0], 128), x.dtype)

    tall = [
        jnp.concatenate(
            [tile(halves[q][h], steps - i if q else i) for h in range(2) for q in range(2)], axis=0
        )
        for i in range(steps + 1)
    ]
    for load in large[1:]:
        load.wait()
    first = jnp.full((half, 128), wave[w * waves], jnp.int32)
    table = []
    for i in range(steps + 1):
        piece = leg[0 if i < steps else 1, :, pl.ds(128 * i if i < steps else 0, 128)]
        if 0 < i < steps:
            other = leg[1, :, pl.ds(128 * (steps - i), 128)]
            piece = jnp.where(first + 128 * i < degrees, piece, other)
        piece = jnp.concatenate(split(piece), axis=0)
        table.append(jnp.concatenate([piece, piece * sign], axis=0))
    fourier = dot(jnp.concatenate(tall, axis=1), jnp.concatenate(table, axis=1), ((1,), (1,)))
    fourier = fourier[:32] + fourier[32:]
    moved = dot(jnp.concatenate(split(fourier), axis=0), pick)
    height = fourier.shape[0]
    moved = moved[:height] + moved[height:]
    slot = iota((16, groups * lanes), 1) % SLOTS == iota((16, groups * lanes), 0) // 2
    message = jnp.zeros((8, groups * lanes), jnp.float32)
    for q in range(waves):
        kept = jnp.where(slot, moved[16 * q : 16 * q + 16], 0.0)
        kept = kept[:8] + kept[8:]
        kept = kept + pltpu.roll(kept, 4, 0)
        kept = kept + pltpu.roll(kept, 2, 0)
        message = jnp.where(iota(message.shape, 0) // 2 == q, kept, message)
    for to in range(groups):
        send[to] = message[:4, to * lanes : (to + 1) * lanes]
    out[g * columns + w] = send[g]

    pl.semaphore_wait(barrier, devices - 1)

    def start(to_g, to_w):
        pltpu.make_async_remote_copy(
            src_ref=send.at[to_g],
            dst_ref=out.at[g * columns + w],
            send_sem=send_sem,
            recv_sem=recv_sem,
            device_id=(to_g, to_w),
            device_id_type=MESH,
        ).start()

    each(start)
    tables(columns, count, segment, wide, wave, points, owner, basis, turn, cross, limit)
    others = out.at[pl.ds(0, devices - 1)]
    pltpu.make_async_copy(others, others, send_sem).wait()
    pltpu.make_async_copy(others, others, recv_sem).wait()


def swap(x):
    even = iota(x.shape, 0) % 2 == 0
    return jnp.where(even, pltpu.roll(x, x.shape[0] - 1, 0), pltpu.roll(x, 1, 0))


def by_field(groups, columns, fields, levels, got):
    depth, lanes = 4 * columns, got.shape[2]
    x = [got[i * columns : (i + 1) * columns].reshape(depth, lanes) for i in range(groups)]
    source = iota((depth, lanes), 1) % SLOTS // levels
    placed = []
    for f in range(fields):
        total = jnp.zeros((depth, lanes), jnp.float32)
        for i in range(groups):
            shift = (i - f) * levels % lanes
            total = jnp.where(source == i, pltpu.roll(x[i], shift, 1) if shift else x[i], total)
        placed.append(total)
    return placed


def arrange(groups, columns, copies, got, coeffs):
    fields, height, _ = coeffs.shape
    depth, lanes = 4 * columns, got.shape[2]
    count = lanes // SLOTS
    level_total = height // count
    levels = level_total // groups
    if level_total == SLOTS:
        same = one_hot(iota((lanes, lanes), 0) == iota((lanes, lanes), 1))
        same = jnp.concatenate([same, same], axis=1)
        for f, x in enumerate(by_field(groups, columns, fields, levels, got)):
            own, other = split(x), split(swap(x))
            source = [jnp.concatenate([own[h]] * copies + [other[h]] * copies, axis=0) for h in range(2)]
            coeffs[f] = dot(same, jnp.concatenate(source, axis=1), ((1,), (1,)))
        return
    x = [got[i * columns : (i + 1) * columns].reshape(depth, lanes) for i in range(groups)]
    x = jnp.concatenate(x, axis=1)
    own, other = split(x), split(swap(x))
    source = [jnp.concatenate([own[h]] * copies + [other[h]] * copies, axis=0) for h in range(2)]
    target = iota((height, 1), 0)
    level = lax.rem(target, level_total)
    for f in range(fields):
        at = (
            lax.div(level, levels) * lanes
            + lax.div(target, level_total) * SLOTS
            + f * levels
            + lax.rem(level, levels)
        )
        move = one_hot(iota((height, groups * lanes), 1) == at)
        coeffs[f] = dot(move, source[0], ((1,), (1,))) + dot(move, source[1], ((1,), (1,)))


def synthesis(groups, columns, got, basis, turn, cross, limit, out, coeffs, grid, out_sem):
    depth = 4 * columns
    count, fields, level_total, segment = grid.shape
    block = fields * level_total
    wide = turn.shape[2]
    copies = wide // depth
    tiles = -(-segment // NEAR)
    arrange(groups, columns, copies, got, coeffs)
    rest = (iota((block * tiles, wide), 1) // depth) % 2 == 1

    def write(p):
        return pltpu.make_async_copy(grid.at[p], out.at[p], out_sem)

    @pl.loop(0, count, unroll=16)
    def _(p):
        at = pl.ds(pl.multiple_of(p * level_total, 8), level_total)
        own = jnp.concatenate([coeffs[f, at, :wide] for f in range(fields)], axis=0)
        other = jnp.concatenate([coeffs[f, at, wide:] for f in range(fields)], axis=0)
        turns, crosses = turn[p], cross[p]
        turned = jnp.concatenate(
            [own * turns[t : t + 1] + other * crosses[t : t + 1] for t in range(tiles)], axis=0
        )
        head = turned.astype(jnp.bfloat16).astype(jnp.float32)
        parts = jnp.where(rest, turned - head, head).astype(jnp.bfloat16)
        high, low = basis[p, :depth], basis[p, depth:]
        values = dot(parts, jnp.concatenate([high, high, low, low][:copies], axis=0))
        room = limit[p]
        room = jnp.concatenate([room] * (level_total // 8), axis=0)
        for start in range(0, segment, 128):
            t, lane = start // NEAR, start % NEAR
            inside = room > start
            for f in range(fields):
                at = t * block + f * level_total
                kept = values[at : at + level_total, lane : lane + 128]
                grid[p, f, :, start : start + 128] = jnp.where(inside, kept, 0.0)
        write(p).start()

    pltpu.make_async_copy(grid, out, out_sem).wait()


def body(groups, columns, spectra, legendre, wave_number, cycle_points, cycle_owner):
    fields, levels, waves, parts, degrees = spectra.shape
    half = legendre.shape[2]
    count = 2 * half // groups
    lanes = count * SLOTS
    level_total = levels * groups
    depth = waves * 2 * columns
    segment = (RMAX + 128 * columns - 1) // (128 * columns) * 128
    wide = -(-3 * depth // 128) * 128
    tile_rows = -(-(-(-segment // NEAR)) // 8) * 8
    vmem, hbm = pl.BlockSpec(memory_space=pltpu.VMEM), pl.BlockSpec(memory_space=pltpu.HBM)
    inputs = (spectra, jnp.swapaxes(legendre, 1, 2), wave_number, cycle_points, cycle_owner)
    handed = pl.pallas_call(
        functools.partial(spread, groups, columns, segment, wide),
        out_shape=[
            pltpu.VMEM((groups * columns, 4, lanes), jnp.float32),
            pltpu.VMEM((count, 2 * depth, NEAR), jnp.bfloat16),
            pltpu.VMEM((count, tile_rows, wide), jnp.float32),
            pltpu.VMEM((count, tile_rows, wide), jnp.float32),
            pltpu.VMEM((count, 8, 128), jnp.int32),
        ],
        in_specs=[hbm] * 5,
        out_specs=[vmem] * 5,
        scratch_shapes=[
            pltpu.VMEM(spectra.shape, jnp.float32),
            pltpu.VMEM((waves, half, degrees), jnp.float32),
            pltpu.SMEM(wave_number.shape, jnp.int32),
            pltpu.SMEM(cycle_points.shape, jnp.int32),
            pltpu.SMEM(cycle_owner.shape, jnp.int32),
            pltpu.VMEM((groups, 4, lanes), jnp.float32),
            pltpu.SemaphoreType.DMA,
            pltpu.SemaphoreType.DMA,
            pltpu.SemaphoreType.DMA((5,)),
        ],
        compiler_params=pltpu.CompilerParams(
            collective_id=0, has_side_effects=True, vmem_limit_bytes=VMEM_BYTES
        ),
        name="spread",
    )(*[pltpu.with_memory_space_constraint(x, pltpu.HBM) for x in inputs])
    return pl.pallas_call(
        functools.partial(synthesis, groups, columns),
        out_shape=jax.ShapeDtypeStruct((count, fields, level_total, segment), jnp.float32),
        in_specs=[vmem] * 5,
        out_specs=pl.BlockSpec(memory_space=pl.ANY),
        scratch_shapes=[
            pltpu.VMEM((fields, count * level_total, 2 * wide), jnp.float32),
            pltpu.VMEM((count, fields, level_total, segment), jnp.float32),
            pltpu.SemaphoreType.DMA,
        ],
        compiler_params=pltpu.CompilerParams(vmem_limit_bytes=VMEM_BYTES),
        name="synthesis",
    )(*[pltpu.with_memory_space_constraint(x, pltpu.VMEM) for x in handed])


def solution(mesh):
    in_specs = (P(None, "grp", "wav", None, None), P("wav", None, None), P(), P(), P())
    out_specs = P("grp", None, None, "wav")
    groups, columns = mesh.shape["grp"], mesh.shape["wav"]
    return jax.shard_map(
        functools.partial(body, groups, columns),
        mesh=mesh,
        in_specs=in_specs,
        out_specs=out_specs,
        check_vma=False,
    )
```

```python
import functools
import math

import jax
import jax.numpy as jnp
from jax import lax
from jax.experimental import pallas as pl
from jax.experimental.pallas import tpu as pltpu
from jax.sharding import PartitionSpec as P

RMAX = 10256
SLOTS = 8
NEAR = 256
VMEM_BYTES = 24000 * 2**10
MESH = pl.DeviceIdType.MESH


def iota(shape, dim):
    return lax.broadcasted_iota(jnp.int32, shape, dim)


def split(x):
    high = x.astype(jnp.bfloat16)
    return high, (x - high.astype(jnp.float32)).astype(jnp.bfloat16)


def dot(a, b, dims=((1,), (0,))):
    return lax.dot_general(a, b, (dims, ((), ())), preferred_element_type=jnp.float32)


def one_hot(mask):
    return mask.astype(jnp.float32).astype(jnp.bfloat16)


def reduced(x, length, inverse):
    turns = jnp.floor(x.astype(jnp.float32) * inverse).astype(jnp.int32)
    left = x - turns * length
    left = jnp.where(left < 0, left + length, left)
    return jnp.where(left >= length, left - length, left)


def cosine(x, length, inverse):
    left = reduced(x, length, inverse)
    left = jnp.where(2 * left > length, left - length, left)
    half = left.astype(jnp.float32) * (inverse * math.pi)
    square = half * half
    series = jnp.full_like(square, 1.0 / math.factorial(13))
    for power in (11, 9, 7, 5, 3, 1):
        sign = -1.0 if power % 4 == 3 else 1.0
        series = series * square + sign / math.factorial(power)
    sine = series * half
    return 1.0 - 2.0 * sine * sine


def routing(owner, half, groups, lanes):
    count = 2 * half // groups
    lane_row = iota((1, count * SLOTS), 1) // SLOTS
    cycles = []
    for to in range(groups):
        cycle = jnp.zeros(lane_row.shape, jnp.int32)
        for row in range(count):
            cycle = jnp.where(lane_row == row, owner[to * count + row], cycle)
        cycles.append(cycle)
    cycle = jnp.concatenate(cycles, axis=1)
    latitude = iota((half, lanes), 0)
    north, south = one_hot(latitude == cycle), one_hot(latitude + half == cycle)
    return jnp.concatenate([north, north, south, south], axis=0)


def tables(columns, count, segment, wide, wave, points, owner, basis, turn, cross, limit):
    depth = 4 * columns
    tile_rows = turn.shape[1]
    g, w = lax.axis_index("grp"), lax.axis_index("wav")
    half = points.shape[0]
    deep = iota((depth, NEAR), 0)
    deep_wave = jnp.zeros((depth, NEAR), jnp.int32)
    across = iota((tile_rows, wide), 1) % depth
    across_wave = jnp.zeros((tile_rows, wide), jnp.int32)
    for q in range(depth // 2):
        deep_wave = jnp.where(deep // 2 == q, wave[q], deep_wave)
        across_wave = jnp.where(across // 2 == q, wave[q], across_wave)
    near = deep_wave * iota((depth, NEAR), 1)
    far = across_wave * (w * segment + NEAR * iota((tile_rows, wide), 0))
    weight = jnp.where(across_wave == 0, 1.0, 2.0)
    point = iota((8, 128), 1) + w * segment

    @pl.loop(0, count, unroll=count if count <= 16 else 1)
    def _(p):
        length = points[lax.rem(owner[g * count + p], half)]
        quarter = lax.div(length, 4)
        inverse = 1.0 / jnp.full((1, 128), length, jnp.int32).astype(jnp.float32)
        across_near = jnp.concatenate([inverse] * (NEAR // 128), axis=1)
        high, low = split(cosine(near + (deep % 2) * quarter, length, across_near))
        basis[p, :depth] = high
        basis[p, depth:] = low
        inverse = jnp.concatenate([inverse] * (wide // 128), axis=1)
        turn[p] = weight * cosine(far, length, inverse)
        cross[p] = weight * cosine(far + (1 + 2 * (across % 2)) * quarter, length, inverse)
        limit[p] = length - point


def spread(groups, columns, segment, wide, *refs):
    spec_in, leg_in, wave_in, points_in, owner_in = refs[:5]
    out, basis, turn, cross, limit = refs[5:10]
    spec, leg, wave, points, owner, send, send_sem, recv_sem, load_sem = refs[10:]
    devices = groups * columns
    g, w = lax.axis_index("grp"), lax.axis_index("wav")
    me = w * groups + g
    waves, half, degrees = leg.shape
    lanes = send.shape[2]
    count = basis.shape[0]
    steps = degrees // 128
    fields, levels = spec_in.shape[:2]
    rows = 2 * fields * levels

    barrier = pltpu.get_barrier_semaphore()
    small = [
        pltpu.make_async_copy(wave_in, wave, load_sem.at[0]),
        pltpu.make_async_copy(points_in, points, load_sem.at[1]),
        pltpu.make_async_copy(owner_in, owner, load_sem.at[2]),
    ]
    large = [pltpu.make_async_copy(spec_in, spec, load_sem.at[3])]
    large.append(pltpu.make_async_copy(leg_in, leg, load_sem.at[4]))
    for load in small + large:
        load.start()

    def each(act):
        @pl.loop(0, devices - 1, unroll=devices - 1 if devices <= 32 else 1)
        def _(i):
            to = i + (me <= i).astype(jnp.int32)
            act(lax.rem(to, groups), lax.div(to, groups))

    each(lambda *to: pl.semaphore_signal(barrier, inc=1, device_id=to, device_id_type=MESH))
    for load in small:
        load.wait()
    pick = routing(owner, half, groups, groups * lanes)
    sign = jnp.where(iota((16, 128), 1) % 2 == 0, 1.0, -1.0).astype(jnp.bfloat16)[:1]
    large[0].wait()
    halves = []
    for q in range(2):
        number = wave[w * waves + q]
        inside = iota((16, degrees), 1) + jnp.where(iota((16, degrees), 0) < rows, number, degrees) < degrees
        x = [spec[f, l, q] for f in range(fields) for l in range(levels)]
        x = jnp.concatenate(x + [jnp.zeros((16 - rows, degrees), jnp.float32)], axis=0)
        halves.append(split(jnp.where(inside, x, 0.0)))

    def tile(x, k):
        if 0 <= k < steps:
            return x[:, 128 * k : 128 * (k + 1)]
        return jnp.zeros((x.shape[0], 128), x.dtype)

    tall = [
        jnp.concatenate(
            [tile(halves[q][h], steps - i if q else i) for h in range(2) for q in range(2)], axis=0
        )
        for i in range(steps + 1)
    ]
    for load in large[1:]:
        load.wait()
    first = jnp.full((half, 128), wave[w * waves], jnp.int32)
    table = []
    for i in range(steps + 1):
        piece = leg[0 if i < steps else 1, :, pl.ds(128 * i if i < steps else 0, 128)]
        if 0 < i < steps:
            other = leg[1, :, pl.ds(128 * (steps - i), 128)]
            piece = jnp.where(first + 128 * i < degrees, piece, other)
        piece = jnp.concatenate(split(piece), axis=0)
        table.append(jnp.concatenate([piece, piece * sign], axis=0))
    fourier = dot(jnp.concatenate(tall, axis=1), jnp.concatenate(table, axis=1), ((1,), (1,)))
    fourier = fourier[:32] + fourier[32:]
    moved = dot(jnp.concatenate(split(fourier), axis=0), pick)
    height = fourier.shape[0]
    moved = moved[:height] + moved[height:]
    turned = (groups - g) * levels if groups * levels == SLOTS else 0
    slot = (iota((16, groups * lanes), 1) + turned) % SLOTS == iota((16, groups * lanes), 0) // 2
    message = jnp.zeros((8, groups * lanes), jnp.float32)
    for q in range(waves):
        kept = jnp.where(slot, moved[16 * q : 16 * q + 16], 0.0)
        kept = kept[:8] + kept[8:]
        kept = kept + pltpu.roll(kept, 4, 0)
        kept = kept + pltpu.roll(kept, 2, 0)
        message = jnp.where(iota(message.shape, 0) // 2 == q, kept, message)
    for to in range(groups):
        send[to] = message[:4, to * lanes : (to + 1) * lanes]
    out[g * columns + w] = send[g]

    pl.semaphore_wait(barrier, devices - 1)

    def start(to_g, to_w):
        pltpu.make_async_remote_copy(
            src_ref=send.at[to_g],
            dst_ref=out.at[g * columns + w],
            send_sem=send_sem,
            recv_sem=recv_sem,
            device_id=(to_g, to_w),
            device_id_type=MESH,
        ).start()

    each(start)
    tables(columns, count, segment, wide, wave, points, owner, basis, turn, cross, limit)
    others = out.at[pl.ds(0, devices - 1)]
    pltpu.make_async_copy(others, others, send_sem).wait()
    pltpu.make_async_copy(others, others, recv_sem).wait()


def swap(x):
    even = iota(x.shape, 0) % 2 == 0
    return jnp.where(even, pltpu.roll(x, x.shape[0] - 1, 0), pltpu.roll(x, 1, 0))


def by_field(groups, columns, fields, levels, got):
    depth, lanes = 4 * columns, got.shape[2]
    x = [got[i * columns : (i + 1) * columns].reshape(depth, lanes) for i in range(groups)]
    source = iota((depth, lanes), 1) % SLOTS // levels
    placed = []
    for f in range(fields):
        total = x[0]
        for i in range(1, groups):
            total = jnp.where(source == (i + f) % groups, x[i], total)
        placed.append(total)
    return placed


def arrange(groups, columns, copies, got, coeffs):
    fields, height, _ = coeffs.shape
    depth, lanes = 4 * columns, got.shape[2]
    count = lanes // SLOTS
    level_total = height // count
    levels = level_total // groups
    if level_total == SLOTS:
        for f, x in enumerate(by_field(groups, columns, fields, levels, got)):
            coeffs[f, :, : copies * depth] = jnp.concatenate([x] * copies, axis=0).T
            coeffs[f, :, copies * depth :] = jnp.concatenate([swap(x)] * copies, axis=0).T
        return
    x = [got[i * columns : (i + 1) * columns].reshape(depth, lanes) for i in range(groups)]
    x = jnp.concatenate(x, axis=1)
    own, other = split(x), split(swap(x))
    source = [jnp.concatenate([own[h]] * copies + [other[h]] * copies, axis=0) for h in range(2)]
    target = iota((height, 1), 0)
    level = lax.rem(target, level_total)
    for f in range(fields):
        at = (
            lax.div(level, levels) * lanes
            + lax.div(target, level_total) * SLOTS
            + f * levels
            + lax.rem(level, levels)
        )
        move = one_hot(iota((height, groups * lanes), 1) == at)
        coeffs[f] = dot(move, source[0], ((1,), (1,))) + dot(move, source[1], ((1,), (1,)))


def synthesis(groups, columns, got, basis, turn, cross, limit, out, coeffs, grid, out_sem):
    depth = 4 * columns
    count, fields, level_total, segment = grid.shape
    block = fields * level_total
    wide = turn.shape[2]
    copies = wide // depth
    tiles = -(-segment // NEAR)
    arrange(groups, columns, copies, got, coeffs)
    rest = (iota((block * tiles, wide), 1) // depth) % 2 == 1

    def write(p):
        return pltpu.make_async_copy(grid.at[p], out.at[p], out_sem)

    @pl.loop(0, count, unroll=16)
    def _(p):
        at = pl.ds(pl.multiple_of(p * level_total, 8), level_total)
        own, other = [], []
        for f in range(fields):
            x = coeffs[f, at, :]
            if level_total == SLOTS and f:
                x = pltpu.roll(x, SLOTS - f * level_total // groups, 0)
            own.append(x[:, :wide])
            other.append(x[:, wide:])
        own, other = jnp.concatenate(own, axis=0), jnp.concatenate(other, axis=0)
        turns, crosses = turn[p], cross[p]
        turned = jnp.concatenate(
            [own * turns[t : t + 1] + other * crosses[t : t + 1] for t in range(tiles)], axis=0
        )
        head = turned.astype(jnp.bfloat16).astype(jnp.float32)
        parts = jnp.where(rest, turned - head, head).astype(jnp.bfloat16)
        high, low = basis[p, :depth], basis[p, depth:]
        values = dot(parts, jnp.concatenate([high, high, low, low][:copies], axis=0))
        room = limit[p]
        room = jnp.concatenate([room] * (level_total // 8), axis=0)
        for start in range(0, segment, 128):
            t, lane = start // NEAR, start % NEAR
            inside = room > start
            for f in range(fields):
                at = t * block + f * level_total
                kept = values[at : at + level_total, lane : lane + 128]
                grid[p, f, :, start : start + 128] = jnp.where(inside, kept, 0.0)
        write(p).start()

    pltpu.make_async_copy(grid, out, out_sem).wait()


def body(groups, columns, spectra, legendre, wave_number, cycle_points, cycle_owner):
    fields, levels, waves, parts, degrees = spectra.shape
    half = legendre.shape[2]
    count = 2 * half // groups
    lanes = count * SLOTS
    level_total = levels * groups
    depth = waves * 2 * columns
    segment = (RMAX + 128 * columns - 1) // (128 * columns) * 128
    wide = -(-3 * depth // 128) * 128
    tile_rows = -(-(-(-segment // NEAR)) // 8) * 8
    vmem, hbm = pl.BlockSpec(memory_space=pltpu.VMEM), pl.BlockSpec(memory_space=pltpu.HBM)
    inputs = (spectra, jnp.swapaxes(legendre, 1, 2), wave_number, cycle_points, cycle_owner)
    handed = pl.pallas_call(
        functools.partial(spread, groups, columns, segment, wide),
        out_shape=[
            pltpu.VMEM((groups * columns, 4, lanes), jnp.float32),
            pltpu.VMEM((count, 2 * depth, NEAR), jnp.bfloat16),
            pltpu.VMEM((count, tile_rows, wide), jnp.float32),
            pltpu.VMEM((count, tile_rows, wide), jnp.float32),
            pltpu.VMEM((count, 8, 128), jnp.int32),
        ],
        in_specs=[hbm] * 5,
        out_specs=[vmem] * 5,
        scratch_shapes=[
            pltpu.VMEM(spectra.shape, jnp.float32),
            pltpu.VMEM((waves, half, degrees), jnp.float32),
            pltpu.SMEM(wave_number.shape, jnp.int32),
            pltpu.SMEM(cycle_points.shape, jnp.int32),
            pltpu.SMEM(cycle_owner.shape, jnp.int32),
            pltpu.VMEM((groups, 4, lanes), jnp.float32),
            pltpu.SemaphoreType.DMA,
            pltpu.SemaphoreType.DMA,
            pltpu.SemaphoreType.DMA((5,)),
        ],
        compiler_params=pltpu.CompilerParams(
            collective_id=0, has_side_effects=True, vmem_limit_bytes=VMEM_BYTES
        ),
        name="spread",
    )(*[pltpu.with_memory_space_constraint(x, pltpu.HBM) for x in inputs])
    return pl.pallas_call(
        functools.partial(synthesis, groups, columns),
        out_shape=jax.ShapeDtypeStruct((count, fields, level_total, segment), jnp.float32),
        in_specs=[vmem] * 5,
        out_specs=pl.BlockSpec(memory_space=pl.ANY),
        scratch_shapes=[
            pltpu.VMEM((fields, count * level_total, 2 * wide), jnp.float32),
            pltpu.VMEM((count, fields, level_total, segment), jnp.float32),
            pltpu.SemaphoreType.DMA,
        ],
        compiler_params=pltpu.CompilerParams(vmem_limit_bytes=VMEM_BYTES),
        name="synthesis",
    )(*[pltpu.with_memory_space_constraint(x, pltpu.VMEM) for x in handed])


def solution(mesh):
    in_specs = (P(None, "grp", "wav", None, None), P("wav", None, None), P(), P(), P())
    out_specs = P("grp", None, None, "wav")
    groups, columns = mesh.shape["grp"], mesh.shape["wav"]
    return jax.shard_map(
        functools.partial(body, groups, columns),
        mesh=mesh,
        in_specs=in_specs,
        out_specs=out_specs,
        check_vma=False,
    )
```

```python
import functools
import math

import jax
import jax.numpy as jnp
from jax import lax
from jax.experimental import pallas as pl
from jax.experimental.pallas import tpu as pltpu
from jax.sharding import PartitionSpec as P

RMAX = 10256
SLOTS = 8
NEAR = 256
VMEM_BYTES = 24000 * 2**10
MESH = pl.DeviceIdType.MESH


def iota(shape, dim):
    return lax.broadcasted_iota(jnp.int32, shape, dim)


def split(x):
    high = x.astype(jnp.bfloat16)
    return high, (x - high.astype(jnp.float32)).astype(jnp.bfloat16)


def dot(a, b, dims=((1,), (0,))):
    return lax.dot_general(a, b, (dims, ((), ())), preferred_element_type=jnp.float32)


def one_hot(mask):
    return mask.astype(jnp.float32).astype(jnp.bfloat16)


def reduced(x, length, inverse):
    turns = jnp.floor(x.astype(jnp.float32) * inverse).astype(jnp.int32)
    left = x - turns * length
    left = jnp.where(left < 0, left + length, left)
    return jnp.where(left >= length, left - length, left)


def cosine(x, length, inverse):
    left = reduced(x, length, inverse)
    left = jnp.where(2 * left > length, left - length, left)
    half = left.astype(jnp.float32) * (inverse * math.pi)
    square = half * half
    series = jnp.full_like(square, 1.0 / math.factorial(13))
    for power in (11, 9, 7, 5, 3, 1):
        sign = -1.0 if power % 4 == 3 else 1.0
        series = series * square + sign / math.factorial(power)
    sine = series * half
    return 1.0 - 2.0 * sine * sine


def routing(owner, half, groups, lanes):
    count = 2 * half // groups
    lane_row = iota((1, count * SLOTS), 1) // SLOTS
    cycles = []
    for to in range(groups):
        cycle = jnp.zeros(lane_row.shape, jnp.int32)
        for row in range(count):
            cycle = jnp.where(lane_row == row, owner[to * count + row], cycle)
        cycles.append(cycle)
    cycle = jnp.concatenate(cycles, axis=1)
    latitude = iota((half, lanes), 0)
    north, south = one_hot(latitude == cycle), one_hot(latitude + half == cycle)
    return jnp.concatenate([north, north, south, south], axis=0)


def tables(columns, count, segment, wide, wave, points, owner, basis, turn, cross, limit):
    depth = 4 * columns
    tile_rows = turn.shape[1]
    g, w = lax.axis_index("grp"), lax.axis_index("wav")
    half = points.shape[0]
    deep = iota((depth, NEAR), 0)
    deep_wave = jnp.zeros((depth, NEAR), jnp.int32)
    across = iota((tile_rows, wide), 1) % depth
    across_wave = jnp.zeros((tile_rows, wide), jnp.int32)
    for q in range(depth // 2):
        deep_wave = jnp.where(deep // 2 == q, wave[q], deep_wave)
        across_wave = jnp.where(across // 2 == q, wave[q], across_wave)
    near = deep_wave * iota((depth, NEAR), 1)
    far = across_wave * (w * segment + NEAR * iota((tile_rows, wide), 0))
    weight = jnp.where(across_wave == 0, 1.0, 2.0)
    point = iota((8, 128), 1) + w * segment

    @pl.loop(0, count, unroll=count if count <= 16 else 1)
    def _(p):
        length = points[lax.rem(owner[g * count + p], half)]
        quarter = lax.div(length, 4)
        inverse = 1.0 / jnp.full((1, 128), length, jnp.int32).astype(jnp.float32)
        across_near = jnp.concatenate([inverse] * (NEAR // 128), axis=1)
        high, low = split(cosine(near + (deep % 2) * quarter, length, across_near))
        basis[p, :depth] = high
        basis[p, depth:] = low
        inverse = jnp.concatenate([inverse] * (wide // 128), axis=1)
        turn[p] = weight * cosine(far, length, inverse)
        cross[p] = weight * cosine(far + (1 + 2 * (across % 2)) * quarter, length, inverse)
        limit[p] = length - point


def spread(groups, columns, segment, wide, *refs):
    spec_in, leg_in, wave_in, points_in, owner_in = refs[:5]
    out, basis, turn, cross, limit = refs[5:10]
    spec, leg, wave, points, owner, send, send_sem, recv_sem, load_sem = refs[10:]
    devices = groups * columns
    g, w = lax.axis_index("grp"), lax.axis_index("wav")
    me = w * groups + g
    waves, half, degrees = leg.shape
    lanes = send.shape[2]
    count = basis.shape[0]
    steps = degrees // 128
    fields, levels = spec_in.shape[:2]
    rows = 2 * fields * levels

    barrier = pltpu.get_barrier_semaphore()
    small = [
        pltpu.make_async_copy(wave_in, wave, load_sem.at[0]),
        pltpu.make_async_copy(points_in, points, load_sem.at[1]),
        pltpu.make_async_copy(owner_in, owner, load_sem.at[2]),
    ]
    large = [pltpu.make_async_copy(spec_in, spec, load_sem.at[3])]
    large.append(pltpu.make_async_copy(leg_in, leg, load_sem.at[4]))
    for load in small + large:
        load.start()

    def each(act):
        @pl.loop(0, devices - 1, unroll=devices - 1 if devices <= 32 else 1)
        def _(i):
            to = i + (me <= i).astype(jnp.int32)
            act(lax.rem(to, groups), lax.div(to, groups))

    each(lambda *to: pl.semaphore_signal(barrier, inc=1, device_id=to, device_id_type=MESH))
    small[0].wait()
    sign = jnp.where(iota((16, 128), 1) % 2 == 0, 1.0, -1.0).astype(jnp.bfloat16)[:1]
    large[0].wait()
    halves = []
    for q in range(2):
        number = wave[w * waves + q]
        inside = iota((16, degrees), 1) + jnp.where(iota((16, degrees), 0) < rows, number, degrees) < degrees
        x = [spec[f, l, q] for f in range(fields) for l in range(levels)]
        x = jnp.concatenate(x + [jnp.zeros((16 - rows, degrees), jnp.float32)], axis=0)
        halves.append(split(jnp.where(inside, x, 0.0)))

    def tile(x, k):
        if 0 <= k < steps:
            return x[:, 128 * k : 128 * (k + 1)]
        return jnp.zeros((x.shape[0], 128), x.dtype)

    tall = [
        jnp.concatenate(
            [tile(halves[q][h], steps - i if q else i) for h in range(2) for q in range(2)], axis=0
        )
        for i in range(steps + 1)
    ]
    for load in large[1:] + small[1:]:
        load.wait()
    pick = routing(owner, half, groups, groups * lanes)
    first = jnp.full((half, 128), wave[w * waves], jnp.int32)
    table = []
    for i in range(steps + 1):
        piece = leg[0 if i < steps else 1, :, pl.ds(128 * i if i < steps else 0, 128)]
        if 0 < i < steps:
            other = leg[1, :, pl.ds(128 * (steps - i), 128)]
            piece = jnp.where(first + 128 * i < degrees, piece, other)
        piece = jnp.concatenate(split(piece), axis=0)
        table.append(jnp.concatenate([piece, piece * sign], axis=0))
    fourier = dot(jnp.concatenate(tall, axis=1), jnp.concatenate(table, axis=1), ((1,), (1,)))
    fourier = fourier[:32] + fourier[32:]
    moved = dot(jnp.concatenate(split(fourier), axis=0), pick)
    height = fourier.shape[0]
    moved = moved[:height] + moved[height:]
    turned = (groups - g) * levels if groups * levels == SLOTS else 0
    slot = (iota((16, groups * lanes), 1) + turned) % SLOTS == iota((16, groups * lanes), 0) // 2
    message = jnp.zeros((8, groups * lanes), jnp.float32)
    for q in range(waves):
        kept = jnp.where(slot, moved[16 * q : 16 * q + 16], 0.0)
        kept = kept[:8] + kept[8:]
        kept = kept + pltpu.roll(kept, 4, 0)
        kept = kept + pltpu.roll(kept, 2, 0)
        message = jnp.where(iota(message.shape, 0) // 2 == q, kept, message)
    for to in range(groups):
        send[to] = message[:4, to * lanes : (to + 1) * lanes]

    pl.semaphore_wait(barrier, devices - 1)

    def start(to_g, to_w):
        pltpu.make_async_remote_copy(
            src_ref=send.at[to_g],
            dst_ref=out.at[g * columns + w],
            send_sem=send_sem,
            recv_sem=recv_sem,
            device_id=(to_g, to_w),
            device_id_type=MESH,
        ).start()

    each(start)
    out[g * columns + w] = send[g]
    tables(columns, count, segment, wide, wave, points, owner, basis, turn, cross, limit)
    others = out.at[pl.ds(0, devices - 1)]
    pltpu.make_async_copy(others, others, send_sem).wait()
    pltpu.make_async_copy(others, others, recv_sem).wait()


def swap(x):
    even = iota(x.shape, 0) % 2 == 0
    return jnp.where(even, pltpu.roll(x, x.shape[0] - 1, 0), pltpu.roll(x, 1, 0))


def by_field(groups, columns, fields, levels, got):
    depth, lanes = 4 * columns, got.shape[2]
    x = [got[i * columns : (i + 1) * columns].reshape(depth, lanes) for i in range(groups)]
    source = iota((depth, lanes), 1) % SLOTS // levels
    placed = []
    for f in range(fields):
        total = x[0]
        for i in range(1, groups):
            total = jnp.where(source == (i + f) % groups, x[i], total)
        placed.append(total)
    return placed


def arrange(groups, columns, copies, got, coeffs):
    fields, height, _ = coeffs.shape
    depth, lanes = 4 * columns, got.shape[2]
    count = lanes // SLOTS
    level_total = height // count
    levels = level_total // groups
    if level_total == SLOTS:
        for f, x in enumerate(by_field(groups, columns, fields, levels, got)):
            coeffs[f, :, : copies * depth] = jnp.concatenate([x] * copies, axis=0).T
            coeffs[f, :, copies * depth :] = jnp.concatenate([swap(x)] * copies, axis=0).T
        return
    x = [got[i * columns : (i + 1) * columns].reshape(depth, lanes) for i in range(groups)]
    x = jnp.concatenate(x, axis=1)
    own, other = split(x), split(swap(x))
    source = [jnp.concatenate([own[h]] * copies + [other[h]] * copies, axis=0) for h in range(2)]
    target = iota((height, 1), 0)
    level = lax.rem(target, level_total)
    for f in range(fields):
        at = (
            lax.div(level, levels) * lanes
            + lax.div(target, level_total) * SLOTS
            + f * levels
            + lax.rem(level, levels)
        )
        move = one_hot(iota((height, groups * lanes), 1) == at)
        coeffs[f] = dot(move, source[0], ((1,), (1,))) + dot(move, source[1], ((1,), (1,)))


def synthesis(groups, columns, got, basis, turn, cross, limit, out, coeffs, grid, out_sem):
    depth = 4 * columns
    count, fields, level_total, segment = grid.shape
    block = fields * level_total
    wide = turn.shape[2]
    copies = wide // depth
    tiles = -(-segment // NEAR)
    arrange(groups, columns, copies, got, coeffs)
    rest = (iota((block * tiles, wide), 1) // depth) % 2 == 1

    def write(p):
        return pltpu.make_async_copy(grid.at[p], out.at[p], out_sem)

    @pl.loop(0, count, unroll=16)
    def _(p):
        at = pl.ds(pl.multiple_of(p * level_total, 8), level_total)
        own, other = [], []
        for f in range(fields):
            x = coeffs[f, at, :]
            if level_total == SLOTS and f:
                x = pltpu.roll(x, SLOTS - f * level_total // groups, 0)
            own.append(x[:, :wide])
            other.append(x[:, wide:])
        own, other = jnp.concatenate(own, axis=0), jnp.concatenate(other, axis=0)
        turns, crosses = turn[p], cross[p]
        turned = jnp.concatenate(
            [own * turns[t : t + 1] + other * crosses[t : t + 1] for t in range(tiles)], axis=0
        )
        head = turned.astype(jnp.bfloat16).astype(jnp.float32)
        parts = jnp.where(rest, turned - head, head).astype(jnp.bfloat16)
        high, low = basis[p, :depth], basis[p, depth:]
        values = dot(parts, jnp.concatenate([high, high, low, low][:copies], axis=0))
        room = limit[p]
        room = jnp.concatenate([room] * (level_total // 8), axis=0)
        for start in range(0, segment, 128):
            t, lane = start // NEAR, start % NEAR
            inside = room > start
            for f in range(fields):
                at = t * block + f * level_total
                kept = values[at : at + level_total, lane : lane + 128]
                grid[p, f, :, start : start + 128] = jnp.where(inside, kept, 0.0)
        write(p).start()

    pltpu.make_async_copy(grid, out, out_sem).wait()


def body(groups, columns, spectra, legendre, wave_number, cycle_points, cycle_owner):
    fields, levels, waves, parts, degrees = spectra.shape
    half = legendre.shape[2]
    count = 2 * half // groups
    lanes = count * SLOTS
    level_total = levels * groups
    depth = waves * 2 * columns
    segment = (RMAX + 128 * columns - 1) // (128 * columns) * 128
    wide = -(-3 * depth // 128) * 128
    tile_rows = -(-(-(-segment // NEAR)) // 8) * 8
    vmem, hbm = pl.BlockSpec(memory_space=pltpu.VMEM), pl.BlockSpec(memory_space=pltpu.HBM)
    inputs = (spectra, jnp.swapaxes(legendre, 1, 2), wave_number, cycle_points, cycle_owner)
    handed = pl.pallas_call(
        functools.partial(spread, groups, columns, segment, wide),
        out_shape=[
            pltpu.VMEM((groups * columns, 4, lanes), jnp.float32),
            pltpu.VMEM((count, 2 * depth, NEAR), jnp.bfloat16),
            pltpu.VMEM((count, tile_rows, wide), jnp.float32),
            pltpu.VMEM((count, tile_rows, wide), jnp.float32),
            pltpu.VMEM((count, 8, 128), jnp.int32),
        ],
        in_specs=[hbm] * 5,
        out_specs=[vmem] * 5,
        scratch_shapes=[
            pltpu.VMEM(spectra.shape, jnp.float32),
            pltpu.VMEM((waves, half, degrees), jnp.float32),
            pltpu.SMEM(wave_number.shape, jnp.int32),
            pltpu.SMEM(cycle_points.shape, jnp.int32),
            pltpu.SMEM(cycle_owner.shape, jnp.int32),
            pltpu.VMEM((groups, 4, lanes), jnp.float32),
            pltpu.SemaphoreType.DMA,
            pltpu.SemaphoreType.DMA,
            pltpu.SemaphoreType.DMA((5,)),
        ],
        compiler_params=pltpu.CompilerParams(
            collective_id=0, has_side_effects=True, vmem_limit_bytes=VMEM_BYTES
        ),
        name="spread",
    )(*[pltpu.with_memory_space_constraint(x, pltpu.HBM) for x in inputs])
    return pl.pallas_call(
        functools.partial(synthesis, groups, columns),
        out_shape=jax.ShapeDtypeStruct((count, fields, level_total, segment), jnp.float32),
        in_specs=[vmem] * 5,
        out_specs=pl.BlockSpec(memory_space=pl.ANY),
        scratch_shapes=[
            pltpu.VMEM((fields, count * level_total, 2 * wide), jnp.float32),
            pltpu.VMEM((count, fields, level_total, segment), jnp.float32),
            pltpu.SemaphoreType.DMA,
        ],
        compiler_params=pltpu.CompilerParams(vmem_limit_bytes=VMEM_BYTES),
        name="synthesis",
    )(*[pltpu.with_memory_space_constraint(x, pltpu.VMEM) for x in handed])


def solution(mesh):
    in_specs = (P(None, "grp", "wav", None, None), P("wav", None, None), P(), P(), P())
    out_specs = P("grp", None, None, "wav")
    groups, columns = mesh.shape["grp"], mesh.shape["wav"]
    return jax.shard_map(
        functools.partial(body, groups, columns),
        mesh=mesh,
        in_specs=in_specs,
        out_specs=out_specs,
        check_vma=False,
    )
```

```python
import functools
import math

import jax
import jax.numpy as jnp
from jax import lax
from jax.experimental import pallas as pl
from jax.experimental.pallas import tpu as pltpu
from jax.sharding import PartitionSpec as P

RMAX = 10256
SLOTS = 8
NEAR = 256
VMEM_BYTES = 24000 * 2**10
MESH = pl.DeviceIdType.MESH


def iota(shape, dim):
    return lax.broadcasted_iota(jnp.int32, shape, dim)


def split(x):
    high = x.astype(jnp.bfloat16)
    return high, (x - high.astype(jnp.float32)).astype(jnp.bfloat16)


def dot(a, b, dims=((1,), (0,))):
    return lax.dot_general(a, b, (dims, ((), ())), preferred_element_type=jnp.float32)


def one_hot(mask):
    return mask.astype(jnp.float32).astype(jnp.bfloat16)


def reduced(x, length, inverse):
    turns = jnp.floor(x.astype(jnp.float32) * inverse).astype(jnp.int32)
    left = x - turns * length
    left = jnp.where(left < 0, left + length, left)
    return jnp.where(left >= length, left - length, left)


def cosine(x, length, inverse):
    left = reduced(x, length, inverse)
    left = jnp.where(2 * left > length, left - length, left)
    half = left.astype(jnp.float32) * (inverse * math.pi)
    square = half * half
    series = jnp.full_like(square, 1.0 / math.factorial(13))
    for power in (11, 9, 7, 5, 3, 1):
        sign = -1.0 if power % 4 == 3 else 1.0
        series = series * square + sign / math.factorial(power)
    sine = series * half
    return 1.0 - 2.0 * sine * sine


def routing(owner, half, groups, lanes):
    count = 2 * half // groups
    lane_row = iota((1, count * SLOTS), 1) // SLOTS
    cycles = []
    for to in range(groups):
        cycle = jnp.zeros(lane_row.shape, jnp.int32)
        for row in range(count):
            cycle = jnp.where(lane_row == row, owner[to * count + row], cycle)
        cycles.append(cycle)
    cycle = jnp.concatenate(cycles, axis=1)
    latitude = iota((half, lanes), 0)
    north, south = one_hot(latitude == cycle), one_hot(latitude + half == cycle)
    return jnp.concatenate([north, north, south, south], axis=0)


def tables(columns, count, segment, wide, wave, points, owner, basis, turn, cross, limit):
    depth = 4 * columns
    tile_rows = turn.shape[1]
    g, w = lax.axis_index("grp"), lax.axis_index("wav")
    half = points.shape[0]
    deep = iota((depth, NEAR), 0)
    deep_wave = jnp.zeros((depth, NEAR), jnp.int32)
    across = iota((tile_rows, wide), 1) % depth
    across_wave = jnp.zeros((tile_rows, wide), jnp.int32)
    for q in range(depth // 2):
        deep_wave = jnp.where(deep // 2 == q, wave[q], deep_wave)
        across_wave = jnp.where(across // 2 == q, wave[q], across_wave)
    near = deep_wave * iota((depth, NEAR), 1)
    far = across_wave * (w * segment + NEAR * iota((tile_rows, wide), 0))
    weight = jnp.where(across_wave == 0, 1.0, 2.0)
    point = iota((8, 128), 1) + w * segment

    @pl.loop(0, count, unroll=count if count <= 16 else 1)
    def _(p):
        length = points[lax.rem(owner[g * count + p], half)]
        quarter = lax.div(length, 4)
        inverse = 1.0 / jnp.full((1, 128), length, jnp.int32).astype(jnp.float32)
        across_near = jnp.concatenate([inverse] * (NEAR // 128), axis=1)
        high, low = split(cosine(near + (deep % 2) * quarter, length, across_near))
        basis[p, :depth] = high
        basis[p, depth:] = low
        inverse = jnp.concatenate([inverse] * (wide // 128), axis=1)
        turn[p] = weight * cosine(far, length, inverse)
        cross[p] = weight * cosine(far + (1 + 2 * (across % 2)) * quarter, length, inverse)
        limit[p] = length - point


def spread(groups, columns, segment, wide, *refs):
    spec_in, leg_in, wave_in, points_in, owner_in = refs[:5]
    out, basis, turn, cross, limit = refs[5:10]
    spec, leg, wave, points, owner, send, send_sem, recv_sem, load_sem = refs[10:]
    devices = groups * columns
    g, w = lax.axis_index("grp"), lax.axis_index("wav")
    me = w * groups + g
    waves, half, degrees = leg.shape
    lanes = send.shape[2]
    count = basis.shape[0]
    steps = degrees // 128
    fields, levels = spec_in.shape[:2]
    rows = 2 * fields * levels

    barrier = pltpu.get_barrier_semaphore()
    small = [
        pltpu.make_async_copy(wave_in, wave, load_sem.at[0]),
        pltpu.make_async_copy(points_in, points, load_sem.at[1]),
        pltpu.make_async_copy(owner_in, owner, load_sem.at[2]),
    ]
    large = [pltpu.make_async_copy(spec_in, spec, load_sem.at[3])]
    large.append(pltpu.make_async_copy(leg_in, leg, load_sem.at[4]))
    for load in small:
        load.start()
    for f in range(spec_in.shape[0]):
        for l in range(spec_in.shape[1]):
            pltpu.make_async_copy(spec_in.at[f, l], spec.at[f, l], load_sem.at[3]).start()
    large[1].start()

    def each(act):
        @pl.loop(0, devices - 1, unroll=devices - 1 if devices <= 32 else 1)
        def _(i):
            to = i + (me <= i).astype(jnp.int32)
            act(lax.rem(to, groups), lax.div(to, groups))

    each(lambda *to: pl.semaphore_signal(barrier, inc=1, device_id=to, device_id_type=MESH))
    small[0].wait()
    sign = jnp.where(iota((16, 128), 1) % 2 == 0, 1.0, -1.0).astype(jnp.bfloat16)[:1]
    large[0].wait()
    halves = []
    for q in range(2):
        number = wave[w * waves + q]
        inside = iota((16, degrees), 1) + jnp.where(iota((16, degrees), 0) < rows, number, degrees) < degrees
        x = [spec[f, l, q] for f in range(fields) for l in range(levels)]
        x = jnp.concatenate(x + [jnp.zeros((16 - rows, degrees), jnp.float32)], axis=0)
        halves.append(split(jnp.where(inside, x, 0.0)))

    def tile(x, k):
        if 0 <= k < steps:
            return x[:, 128 * k : 128 * (k + 1)]
        return jnp.zeros((x.shape[0], 128), x.dtype)

    tall = [
        jnp.concatenate(
            [tile(halves[q][h], steps - i if q else i) for h in range(2) for q in range(2)], axis=0
        )
        for i in range(steps + 1)
    ]
    for load in large[1:] + small[1:]:
        load.wait()
    pick = routing(owner, half, groups, groups * lanes)
    first = jnp.full((half, 128), wave[w * waves], jnp.int32)
    table = []
    for i in range(steps + 1):
        piece = leg[0 if i < steps else 1, :, pl.ds(128 * i if i < steps else 0, 128)]
        if 0 < i < steps:
            other = leg[1, :, pl.ds(128 * (steps - i), 128)]
            piece = jnp.where(first + 128 * i < degrees, piece, other)
        piece = jnp.concatenate(split(piece), axis=0)
        table.append(jnp.concatenate([piece, piece * sign], axis=0))
    fourier = dot(jnp.concatenate(tall, axis=1), jnp.concatenate(table, axis=1), ((1,), (1,)))
    fourier = fourier[:32] + fourier[32:]
    moved = dot(jnp.concatenate(split(fourier), axis=0), pick)
    height = fourier.shape[0]
    moved = moved[:height] + moved[height:]
    turned = (groups - g) * levels if groups * levels == SLOTS else 0
    slot = (iota((16, groups * lanes), 1) + turned) % SLOTS == iota((16, groups * lanes), 0) // 2
    message = jnp.zeros((8, groups * lanes), jnp.float32)
    for q in range(waves):
        kept = jnp.where(slot, moved[16 * q : 16 * q + 16], 0.0)
        kept = kept[:8] + kept[8:]
        kept = kept + pltpu.roll(kept, 4, 0)
        kept = kept + pltpu.roll(kept, 2, 0)
        message = jnp.where(iota(message.shape, 0) // 2 == q, kept, message)
    for to in range(groups):
        send[to] = message[:4, to * lanes : (to + 1) * lanes]

    pl.semaphore_wait(barrier, devices - 1)

    def start(to_g, to_w):
        pltpu.make_async_remote_copy(
            src_ref=send.at[to_g],
            dst_ref=out.at[g * columns + w],
            send_sem=send_sem,
            recv_sem=recv_sem,
            device_id=(to_g, to_w),
            device_id_type=MESH,
        ).start()

    each(start)
    out[g * columns + w] = send[g]
    tables(columns, count, segment, wide, wave, points, owner, basis, turn, cross, limit)
    others = out.at[pl.ds(0, devices - 1)]
    pltpu.make_async_copy(others, others, send_sem).wait()
    pltpu.make_async_copy(others, others, recv_sem).wait()


def swap(x):
    even = iota(x.shape, 0) % 2 == 0
    return jnp.where(even, pltpu.roll(x, x.shape[0] - 1, 0), pltpu.roll(x, 1, 0))


def by_field(groups, columns, fields, levels, got):
    depth, lanes = 4 * columns, got.shape[2]
    x = [got[i * columns : (i + 1) * columns].reshape(depth, lanes) for i in range(groups)]
    source = iota((depth, lanes), 1) % SLOTS // levels
    placed = []
    for f in range(fields):
        total = x[0]
        for i in range(1, groups):
            total = jnp.where(source == (i + f) % groups, x[i], total)
        placed.append(total)
    return placed


def arrange(groups, columns, copies, got, coeffs):
    fields, height, _ = coeffs.shape
    depth, lanes = 4 * columns, got.shape[2]
    count = lanes // SLOTS
    level_total = height // count
    levels = level_total // groups
    if level_total == SLOTS:
        for f, x in enumerate(by_field(groups, columns, fields, levels, got)):
            coeffs[f, :, : copies * depth] = jnp.concatenate([x] * copies, axis=0).T
            coeffs[f, :, copies * depth :] = jnp.concatenate([swap(x)] * copies, axis=0).T
        return
    x = [got[i * columns : (i + 1) * columns].reshape(depth, lanes) for i in range(groups)]
    x = jnp.concatenate(x, axis=1)
    own, other = split(x), split(swap(x))
    source = [jnp.concatenate([own[h]] * copies + [other[h]] * copies, axis=0) for h in range(2)]
    target = iota((height, 1), 0)
    level = lax.rem(target, level_total)
    for f in range(fields):
        at = (
            lax.div(level, levels) * lanes
            + lax.div(target, level_total) * SLOTS
            + f * levels
            + lax.rem(level, levels)
        )
        move = one_hot(iota((height, groups * lanes), 1) == at)
        coeffs[f] = dot(move, source[0], ((1,), (1,))) + dot(move, source[1], ((1,), (1,)))


def synthesis(groups, columns, got, basis, turn, cross, limit, out, coeffs, grid, out_sem):
    depth = 4 * columns
    count, fields, level_total, segment = grid.shape
    block = fields * level_total
    wide = turn.shape[2]
    copies = wide // depth
    tiles = -(-segment // NEAR)
    arrange(groups, columns, copies, got, coeffs)
    rest = (iota((block * tiles, wide), 1) // depth) % 2 == 1

    def write(p):
        return pltpu.make_async_copy(grid.at[p], out.at[p], out_sem)

    @pl.loop(0, count, unroll=16)
    def _(p):
        at = pl.ds(pl.multiple_of(p * level_total, 8), level_total)
        own, other = [], []
        for f in range(fields):
            x = coeffs[f, at, :]
            if level_total == SLOTS and f:
                x = pltpu.roll(x, SLOTS - f * level_total // groups, 0)
            own.append(x[:, :wide])
            other.append(x[:, wide:])
        own, other = jnp.concatenate(own, axis=0), jnp.concatenate(other, axis=0)
        turns, crosses = turn[p], cross[p]
        turned = jnp.concatenate(
            [own * turns[t : t + 1] + other * crosses[t : t + 1] for t in range(tiles)], axis=0
        )
        head = turned.astype(jnp.bfloat16).astype(jnp.float32)
        parts = jnp.where(rest, turned - head, head).astype(jnp.bfloat16)
        high, low = basis[p, :depth], basis[p, depth:]
        values = dot(parts, jnp.concatenate([high, high, low, low][:copies], axis=0))
        room = limit[p]
        room = jnp.concatenate([room] * (level_total // 8), axis=0)
        for start in range(0, segment, 128):
            t, lane = start // NEAR, start % NEAR
            inside = room > start
            for f in range(fields):
                at = t * block + f * level_total
                kept = values[at : at + level_total, lane : lane + 128]
                grid[p, f, :, start : start + 128] = jnp.where(inside, kept, 0.0)
        write(p).start()

    pltpu.make_async_copy(grid, out, out_sem).wait()


def body(groups, columns, spectra, legendre, wave_number, cycle_points, cycle_owner):
    fields, levels, waves, parts, degrees = spectra.shape
    half = legendre.shape[2]
    count = 2 * half // groups
    lanes = count * SLOTS
    level_total = levels * groups
    depth = waves * 2 * columns
    segment = (RMAX + 128 * columns - 1) // (128 * columns) * 128
    wide = -(-3 * depth // 128) * 128
    tile_rows = -(-(-(-segment // NEAR)) // 8) * 8
    vmem, hbm = pl.BlockSpec(memory_space=pltpu.VMEM), pl.BlockSpec(memory_space=pltpu.HBM)
    inputs = (spectra, jnp.swapaxes(legendre, 1, 2), wave_number, cycle_points, cycle_owner)
    handed = pl.pallas_call(
        functools.partial(spread, groups, columns, segment, wide),
        out_shape=[
            pltpu.VMEM((groups * columns, 4, lanes), jnp.float32),
            pltpu.VMEM((count, 2 * depth, NEAR), jnp.bfloat16),
            pltpu.VMEM((count, tile_rows, wide), jnp.float32),
            pltpu.VMEM((count, tile_rows, wide), jnp.float32),
            pltpu.VMEM((count, 8, 128), jnp.int32),
        ],
        in_specs=[hbm] * 5,
        out_specs=[vmem] * 5,
        scratch_shapes=[
            pltpu.VMEM(spectra.shape, jnp.float32),
            pltpu.VMEM((waves, half, degrees), jnp.float32),
            pltpu.SMEM(wave_number.shape, jnp.int32),
            pltpu.SMEM(cycle_points.shape, jnp.int32),
            pltpu.SMEM(cycle_owner.shape, jnp.int32),
            pltpu.VMEM((groups, 4, lanes), jnp.float32),
            pltpu.SemaphoreType.DMA,
            pltpu.SemaphoreType.DMA,
            pltpu.SemaphoreType.DMA((5,)),
        ],
        compiler_params=pltpu.CompilerParams(
            collective_id=0, has_side_effects=True, vmem_limit_bytes=VMEM_BYTES
        ),
        name="spread",
    )(*[pltpu.with_memory_space_constraint(x, pltpu.HBM) for x in inputs])
    return pl.pallas_call(
        functools.partial(synthesis, groups, columns),
        out_shape=jax.ShapeDtypeStruct((count, fields, level_total, segment), jnp.float32),
        in_specs=[vmem] * 5,
        out_specs=pl.BlockSpec(memory_space=pl.ANY),
        scratch_shapes=[
            pltpu.VMEM((fields, count * level_total, 2 * wide), jnp.float32),
            pltpu.VMEM((count, fields, level_total, segment), jnp.float32),
            pltpu.SemaphoreType.DMA,
        ],
        compiler_params=pltpu.CompilerParams(vmem_limit_bytes=VMEM_BYTES),
        name="synthesis",
    )(*[pltpu.with_memory_space_constraint(x, pltpu.VMEM) for x in handed])


def solution(mesh):
    in_specs = (P(None, "grp", "wav", None, None), P("wav", None, None), P(), P(), P())
    out_specs = P("grp", None, None, "wav")
    groups, columns = mesh.shape["grp"], mesh.shape["wav"]
    return jax.shard_map(
        functools.partial(body, groups, columns),
        mesh=mesh,
        in_specs=in_specs,
        out_specs=out_specs,
        check_vma=False,
    )
```
